512 devices in a mesh: sub: 32 (over z, core), blk: 16 (over y, x).
Axes of the slice: x: 4, y: 4, z: 16, core: 2. Of those that a mesh axis runs over, the one named last changes fastest.
Arguments:
- impedance: bfloat16 [32, 16384, 1024], P('sub', 'blk'), may hold values from -0.1875 to 0.1875
- port_node: int32 [32, 1024], P('sub', 'blk'), may hold values from 0 to 16383, as said below
- far_system: int32 [32, 1024], P('sub', 'blk'), may hold values from 0 to 31, as said below
- delays: int32 [32, 1024], P('sub', 'blk'), may hold values from 2 to 4, as said below
- admittance: float32 [32, 1024], P('sub', 'blk'), may hold values from 0.5 to 2
- pole_rates: float32 [32, 12, 1024], P('sub', None, 'blk'), may hold values from 0.05 to 0.95
- residues: float32 [32, 12, 1024], P('sub', None, 'blk'), may hold values from -1.8 to 1.8
- states: float32 [32, 12, 1024, 256], P('sub', None, 'blk'), may hold values from -3 to 3
- history: float32 [32, 4, 1024, 256], P('sub', None, 'blk'), may hold values from -6 to 6
- event_port: int32 [32, 256], P('sub'), may hold values from 0 to 1023
- amplitude: float32 [32, 2, 256], P('sub'), may hold values from -48 to 48
Outputs:
- peak_voltage: bfloat16 [32, 16384, 256], P('sub', 'blk')
- new_states: float32 [32, 12, 1024, 256], P('sub', None, 'blk')
- arrived: float32 [32, 1024, 2, 256], P('sub', 'blk')
The draws below stay inside these ranges and needn't reach their ends.
Inputs may be any that keep to these rules, and one draw needn't show every extreme that they name: `port_node`: the node of terminal j lies in rows (j // 64) * 1024 to (j // 64 + 1) * 1024 - 1; the terminals of one subsystem have distinct nodes. Line j joins terminal j of two different subsystems: far_system[far_system[s, j], j] = s and far_system[s, j] != s. Of the terminals b * 64 to (b + 1) * 64 - 1 of one subsystem at most 6 lead to one same subsystem, and in every such group exactly 6 do for one of them. delays[s, j] = delays[far_system[s, j], j].
All inputs are finite; a program needn't handle non-finite values.
Results may differ from the reference program's by a relative error of at most 0.0042.
Values may be sent and summed in bfloat16 or wider, within the bound.
A program may use at most 64 MiB of HBM per device.

```python
import math
import jax
import jax.numpy as jnp
from jax import lax

NODES = 16384
PORTS = 1024
POLES = 12
STEPS = 2
DEPTH = 4
SCEN = 256
SUBS = 32
NB = 1024
PB = 64


def line_offsets(key):
    groups = PORTS // PB
    spread = SUBS - 1
    surplus = max(1, PB // 16)

    def one_group(group_key):
        order = jax.random.permutation(jax.random.fold_in(group_key, 1), PB)
        labels = jax.random.permutation(jax.random.fold_in(group_key, 2), spread)
        classes = jnp.where(order < PB - surplus, order % spread, 0)
        return 1 + labels[classes]
    group_keys = jax.random.split(jax.random.fold_in(key, 11), groups)
    return jax.vmap(one_group)(group_keys).reshape(PORTS).astype(jnp.int32)


def draw_far_system(key, part):
    offsets = line_offsets(key)
    systems = jnp.arange(SUBS, dtype=jnp.int32)
    return jnp.bitwise_xor(systems[:, None], offsets[None, :]).astype(jnp.int32)


def draw_delays(key, part):
    partners = draw_far_system(key, part)
    row_keys = jax.random.split(jax.random.fold_in(key, 23), SUBS)

    def one_row(row_key):
        return jax.random.permutation(row_key, PORTS)
    orders = jax.vmap(one_row)(row_keys)
    base = STEPS + orders % (DEPTH - STEPS + 1)
    lower = jnp.minimum(jnp.arange(SUBS, dtype=jnp.int32)[:, None], partners)
    return base[lower, jnp.arange(PORTS, dtype=jnp.int32)[None, :]].astype(jnp.int32)


def draw_port_node(key, part):
    groups = PORTS // PB
    group_keys = jax.random.split(jax.random.fold_in(key, 37), SUBS * groups)

    def one_group(group_key):
        inner = jax.random.permutation(jax.random.fold_in(group_key, 1), NB - 2)[:PB - 2] + 1
        ends = jnp.array([0, NB - 1], dtype=jnp.int32)
        together = jnp.concatenate([ends, inner.astype(jnp.int32)])
        return jax.random.permutation(jax.random.fold_in(group_key, 2), together)
    picked = jax.vmap(one_group)(group_keys).reshape(SUBS, groups, PB)
    offsets = (jnp.arange(groups, dtype=jnp.int32) * NB)[None, :, None]
    return (picked + offsets).reshape(SUBS, PORTS).astype(jnp.int32)


def place_ends(drawn, own_key, smallest, high):
    shape = drawn.shape
    index_at = [jax.random.randint(jax.random.fold_in(own_key, axis), (), 0, shape[axis]) for axis in range(len(shape))]
    drawn = drawn.at[tuple(index_at)].set(smallest)
    longest = shape.index(max(shape))
    index_at[longest] = (index_at[longest] + 1) % shape[longest]
    return drawn.at[tuple(index_at)].set(high)


def steps_of(stream_key, dims, cuts, least, largest):
    def one(axis_at, shards_of):
        draws = jax.random.uniform(jax.random.fold_in(jax.random.fold_in(stream_key, 6), axis_at), (shards_of,), jnp.float32, least / len(cuts), largest / len(cuts))
        return jnp.repeat(jnp.exp(draws), dims[axis_at] // shards_of).reshape((-1,) + (1,) * (len(dims) - axis_at - 1))

    factor_of = one(*cuts[0])
    for cut in cuts[1:]:
        factor_of = factor_of * one(*cut)
    return factor_of


def gaussian(key, extent, deviation, reach, pieces=(), held_as=jnp.bfloat16):
    level = steps_of(key, extent, pieces, -0.22, 0.18) if pieces else 1.0
    values = jax.random.normal(key, extent, jnp.float32) * deviation * level
    return jnp.minimum(jnp.maximum(values, -reach), reach).astype(held_as)


def setup_inputs(seed: int = 0) -> dict:
    splits = jax.random.split(jax.random.key(seed), 12)
    impedance = gaussian(splits[0], (SUBS, NODES, PORTS), PORTS ** -0.5, 0.1875, ((0, 32), (1, 16)))
    port_node = draw_port_node(jax.random.fold_in(splits[11], 71), 0)
    far_system = draw_far_system(jax.random.fold_in(splits[11], 71), 0)
    delays = draw_delays(jax.random.fold_in(splits[11], 71), 0)
    admittance = jnp.clip(jnp.exp(math.log(2.0) - 1.3862944 * jax.random.uniform(splits[4], (SUBS, PORTS), jnp.float32) ** steps_of(splits[4], (SUBS, PORTS), ((0, 32), (1, 16)), -0.2, 0.2)), 0.5, 2.0)
    pole_rates = jnp.clip(jnp.exp(math.log(0.95) - 2.944439 * jax.random.uniform(splits[5], (SUBS, POLES, PORTS), jnp.float32) ** steps_of(splits[5], (SUBS, POLES, PORTS), ((0, 32), (2, 16)), -0.2, 0.2)), 0.05, 0.95)
    residues = gaussian(splits[6], (SUBS, POLES, PORTS), 0.3, 1.8, ((0, 32), (2, 16)), jnp.float32)
    states = gaussian(splits[7], (SUBS, POLES, PORTS, SCEN), 0.5, 3.0, ((0, 32), (2, 16)), jnp.float32)
    history = gaussian(splits[8], (SUBS, DEPTH, PORTS, SCEN), 1.0, 6.0, ((0, 32), (2, 16)), jnp.float32)
    event_port = place_ends(jax.random.randint(splits[9], (SUBS, SCEN), 0, PORTS), jax.random.fold_in(splits[9], 1), 0, PORTS - 1).astype(jnp.int32)
    amplitude = gaussian(splits[10], (SUBS, STEPS, SCEN), 8.0, 48.0, ((0, 32),), jnp.float32)
    return dict(impedance=impedance, port_node=port_node, far_system=far_system, delays=delays, admittance=admittance, pole_rates=pole_rates, residues=residues, states=states, history=history, event_port=event_port, amplitude=amplitude)


def pick_incident(history, delays, step_index):
    depth_iota = jnp.arange(history.shape[0], dtype=jnp.int32)
    wanted = delays - step_index - 1
    chosen = jnp.where(wanted[None, :, None] == depth_iota[:, None, None], history, 0.0)
    return jnp.sum(chosen, axis=0)


def subsystem(operands):
    impedance, port_node, delays, admittance, pole_rates, residues, states, history, event_port, amplitude = operands
    port_index = jnp.arange(PORTS, dtype=jnp.int32)
    current = states
    peak_value = jnp.zeros((NODES, SCEN), jnp.float32)
    emitted = []
    for step_index in range(STEPS):
        incident = pick_incident(history, delays, step_index)
        current = pole_rates[:, :, None] * current + residues[:, :, None] * incident[None]
        source = jnp.sum(current, axis=0)
        switched = jnp.where(event_port[None, :] == port_index[:, None], amplitude[step_index][None, :], 0.0)
        injection = (source + switched).astype(jnp.bfloat16)
        voltage = jnp.dot(impedance, injection, preferred_element_type=jnp.float32)
        peak_value = jnp.maximum(peak_value, jnp.abs(voltage))
        emitted.append(2.0 * admittance[:, None] * voltage[port_node] - source)
    return peak_value.astype(jnp.bfloat16), current, jnp.stack(emitted, axis=1)


def reference(impedance, port_node, far_system, delays, admittance, pole_rates, residues, states, history, event_port, amplitude):
    peak_voltage, new_states, emitted = lax.map(subsystem, (impedance, port_node, delays, admittance, pole_rates, residues, states, history, event_port, amplitude))
    port_index = jnp.arange(PORTS, dtype=jnp.int32)
    arrived = emitted[far_system, port_index[None, :]]
    return peak_voltage, new_states, arrived
```

```python
import functools

import jax
import jax.numpy as jnp
from jax import lax
from jax.experimental import pallas as pl
from jax.experimental.pallas import tpu as pltpu
from jax.sharding import PartitionSpec as P

MESH = pl.DeviceIdType.MESH
F32, BF16, I32 = jnp.float32, jnp.bfloat16, jnp.int32

SUBS, SIDE, PB, COLS, POLES, DEPTH, STEPS = 32, 4, 64, 256, 12, 4, 2
CAP = 6
SLOT = CAP * STEPS * 2


def kernel(
    z_hbm, port_hbm, far_hbm, delay_hbm, adm_hbm, rate_hbm, res_hbm, state_hbm, hist_hbm, event_hbm, amp_hbm,
    peak_hbm, new_hbm, arr_hbm,
    z_v, port_v, far_v, delay_v, adm_v, rate_v, res_v, state_v, hist_v, event_v, amp_v,
    peak_ref, new_ref, arr_ref, table, gath, source, ports, outbox, inbox,
    in_sem, done_sem, s1, r1, s2, r2, s3, r3, s4, r4, out_sem, box_sem,
):
    sub = lax.axis_index("sub")
    blk = lax.axis_index("blk")
    x = lax.rem(blk, SIDE)
    y = lax.div(blk, SIDE)
    xs = (lax.rem(x + 3, SIDE), lax.rem(x + 1, SIDE))
    ys = (lax.rem(y + 3, SIDE), lax.rem(y + 1, SIDE))
    by_x = tuple(y * SIDE + v for v in xs)
    by_y = tuple(v * SIDE + x for v in ys)

    loads = {}
    pairs = (
        (port_hbm, port_v), (far_hbm, far_v), (delay_hbm, delay_v), (adm_hbm, adm_v), (rate_hbm, rate_v),
        (res_hbm, res_v), (event_hbm, event_v), (amp_hbm, amp_v), (hist_hbm, hist_v), (state_hbm, state_v), (z_hbm, z_v),
    )
    for n, (src, dst) in enumerate(pairs):
        loads[n] = pltpu.make_async_copy(src, dst, in_sem.at[n])
        loads[n].start()

    barrier = pltpu.get_barrier_semaphore()
    for b in by_x + by_y:
        pl.semaphore_signal(barrier, inc=1, device_id=(sub, b), device_id_type=MESH)

    def greet(k, c):
        pl.semaphore_signal(barrier, inc=1, device_id=(lax.rem(sub + k, SUBS), blk), device_id_type=MESH)
        return c

    lax.fori_loop(1, SUBS, greet, 0)

    for n in range(8):
        loads[n].wait()
    table[...] = jnp.zeros_like(table)
    table[0:POLES, 0:PB] = rate_v[:, 0, :]
    table[16:16 + POLES, 0:PB] = res_v[:, 0, :]
    table[32:33, 0:PB] = adm_v[...]
    table[33:34, 0:PB] = far_v[...].astype(F32)
    table[34:35, 0:PB] = (port_v[...] - blk * 1024).astype(F32)
    table[35:36, 0:PB] = delay_v[...].astype(F32)
    turned = jnp.transpose(table[...])

    loads[8].wait()
    loads[9].wait()
    for part in range(4):
        rows = slice(part * 16, part * 16 + 16)
        delay = turned[rows, 35:36]
        arrive = []
        for step in range(STEPS):
            got = jnp.zeros((16, COLS), F32)
            for d in range(DEPTH):
                got = jnp.where(delay == float(d + step + 1), hist_v[0, d, rows, :], got)
            arrive.append(got)
        totals = [jnp.zeros((16, COLS), F32) for _ in range(STEPS)]
        for p in range(POLES):
            rate = turned[rows, p:p + 1]
            weight = turned[rows, 16 + p:17 + p]
            now = state_v[0, p, rows, :]
            for step in range(STEPS):
                now = rate * now + weight * arrive[step]
                totals[step] = totals[step] + now
            new_ref[0, p, rows, :] = now
        index = lax.broadcasted_iota(I32, (16, COLS), 0) + (blk * PB + part * 16)
        hit = event_v[...] == index
        for step in range(STEPS):
            source[step, rows, :] = totals[step]
            kick = jnp.where(hit, amp_v[0, step:step + 1, :], 0.0)
            gath[step, y, pl.ds(pl.multiple_of(x * PB + part * 16, 16), 16), :] = (totals[step] + kick).astype(BF16)

    stores = [pltpu.make_async_copy(new_ref, new_hbm, done_sem.at[0])]
    stores[0].start()
    pl.semaphore_wait(barrier, 4 + SUBS - 1)

    def send(src, peer, s, r):
        c = pltpu.make_async_remote_copy(
            src_ref=src, dst_ref=src, send_sem=s, recv_sem=r, device_id=(sub, peer), device_id_type=MESH)
        c.start()
        return c

    def slab(step, yy, xx, lo, n):
        return gath.at[step, yy, pl.ds(pl.multiple_of(xx * PB + lo, 16), n), :]

    near = (by_x, by_y)
    far = (by_y, by_x)
    c1 = [[send(slab(t, y, x, 0, PB), near[t][1 - w], s1.at[t, w], r1.at[t, w]) for w in range(2)] for t in range(2)]

    far_row = far_v[...].astype(F32)
    far_col = turned[0:PB, 33:34]
    node_col = turned[0:PB, 34:35]
    same = far_col == far_row
    ii = lax.broadcasted_iota(I32, (PB, PB), 0)
    jj = lax.broadcasted_iota(I32, (PB, PB), 1)
    rank_row = jnp.sum(jnp.where(same & (ii < jj), 1.0, 0.0), axis=0, keepdims=True)
    rank_col = jnp.sum(jnp.where(same & (jj < ii), 1.0, 0.0), axis=1, keepdims=True)
    slot_row = (far_row * SLOT + rank_row).astype(I32)
    slot_col = (far_col * SLOT + rank_col).astype(I32)
    place_row = jnp.concatenate([slot_row + q * CAP for q in range(4)], axis=1)
    place_col = jnp.concatenate([slot_col + q * CAP for q in range(4)], axis=0)
    pick = (lax.broadcasted_iota(I32, (PB, 1024), 1) == node_col.astype(I32)).astype(BF16)

    c2 = [[None, None], [None, None]]
    for t in range(2):
        for w in range(2):
            c1[t][w].wait_recv()
            yy, xx = (y, xs[w]) if t == 0 else (ys[w], x)
            c2[t][w] = send(slab(t, yy, xx, 32 * w, 32), near[t][1 - w], s2.at[t, w], r2.at[t, w])

    loads[10].wait()
    ports[...] = jnp.dot(pick, z_v[0], preferred_element_type=F32).astype(BF16)

    c3 = [[None, None], [None, None]]
    for t in range(2):
        for w in range(2):
            c2[t][w].wait_recv()
        line = gath.at[0, y] if t == 0 else gath.at[1, :, pl.ds(pl.multiple_of(x * PB, 16), PB), :]
        for w in range(2):
            c3[t][w] = send(line, far[t][1 - w], s3.at[t, w], r3.at[t, w])
    c4 = [[None, None], [None, None]]
    for t in range(2):
        for w in range(2):
            c3[t][w].wait_recv()
            if t == 0:
                half = gath.at[0, ys[w], pl.ds(128 * w, 128), :]
            else:
                half = gath.at[1, pl.ds(2 * w, 2), pl.ds(pl.multiple_of(xs[w] * PB, 16), PB), :]
            c4[t][w] = send(half, far[t][1 - w], s4.at[t, w], r4.at[t, w])
    for t in range(2):
        for w in range(2):
            c4[t][w].wait_recv()

    twice = 2.0 * turned[0:PB, 32:33]
    waves = []
    for t in range(2):
        volt = jnp.dot(ports[...], gath[t].reshape(1024, COLS), preferred_element_type=F32)
        wave = (twice * volt - source[t]).astype(BF16)
        waves += [wave[:, 0:128], wave[:, 128:256]]
    stacked = jnp.concatenate(waves, axis=0)
    pack = (lax.broadcasted_iota(I32, (SUBS * SLOT, 256), 0) == place_row).astype(BF16)
    boxes = jnp.dot(pack, stacked, preferred_element_type=F32).astype(BF16)
    outbox[...] = boxes.reshape(SUBS, SLOT, 128)

    def box(k):
        d = lax.rem(sub + k, SUBS)
        return pltpu.make_async_remote_copy(
            src_ref=outbox.at[d], dst_ref=inbox.at[sub], send_sem=out_sem.at[d], recv_sem=box_sem.at[sub],
            device_id=(d, blk), device_id_type=MESH)

    box(16).start()

    def post(i, c):
        box(15 - i).start()
        box(17 + i).start()
        return c

    lax.fori_loop(0, 15, post, 0)
    inbox[sub] = jnp.zeros((SLOT, 128), BF16)

    for part in range(4):
        rows = slice(part * 256, part * 256 + 256)
        v0 = jnp.dot(z_v[0, rows, :], gath[0].reshape(1024, COLS), preferred_element_type=F32)
        v1 = jnp.dot(z_v[0, rows, :], gath[1].reshape(1024, COLS), preferred_element_type=F32)
        peak_ref[0, rows, :] = jnp.maximum(jnp.abs(v0), jnp.abs(v1)).astype(BF16)

    stores.append(pltpu.make_async_copy(peak_ref, peak_hbm, done_sem.at[1]))
    stores[1].start()
    unpack = (lax.broadcasted_iota(I32, (256, SUBS * SLOT), 1) == place_col).astype(BF16)

    def collect(k, c):
        d = lax.rem(sub + k, SUBS)
        pltpu.make_async_remote_copy(
            src_ref=outbox.at[d], dst_ref=inbox.at[d], send_sem=out_sem.at[d], recv_sem=box_sem.at[d],
            device_id=(d, blk), device_id_type=MESH).wait_recv()
        return c

    lax.fori_loop(1, SUBS, collect, 0)
    got = jnp.dot(unpack, inbox[...].reshape(SUBS * SLOT, 128), preferred_element_type=F32)
    for t in range(2):
        arr_ref[0, :, t, 0:128] = got[128 * t:128 * t + PB]
        arr_ref[0, :, t, 128:256] = got[128 * t + PB:128 * t + 2 * PB]
    stores.append(pltpu.make_async_copy(arr_ref, arr_hbm, done_sem.at[2]))
    stores[2].start()

    for t in range(2):
        for w in range(2):
            for c in (c1, c2, c3, c4):
                c[t][w].wait_send()

    def drain(k, c):
        box(k).wait_send()
        return c

    lax.fori_loop(1, SUBS, drain, 0)
    for c in stores:
        c.wait()


def body(*args):
    args = list(args)
    for n in (5, 6):
        args[n] = args[n].reshape(POLES, 1, PB)
    dma = pltpu.SemaphoreType.DMA
    outs = (
        jax.ShapeDtypeStruct((1, 1024, COLS), BF16),
        jax.ShapeDtypeStruct((1, POLES, PB, COLS), F32),
        jax.ShapeDtypeStruct((1, PB, STEPS, COLS), F32),
    )
    return pl.pallas_call(
        kernel,
        out_shape=outs,
        in_specs=[pl.BlockSpec(memory_space=pltpu.HBM)] * len(args),
        out_specs=[pl.BlockSpec(memory_space=pltpu.HBM)] * 3,
        scratch_shapes=[pltpu.VMEM(a.shape, a.dtype) for a in (*args, *outs)] + [
            pltpu.VMEM((128, 128), F32),
            pltpu.VMEM((2, SIDE, SIDE * PB, COLS), BF16),
            pltpu.VMEM((2, PB, COLS), F32),
            pltpu.VMEM((PB, 1024), BF16),
            pltpu.VMEM((SUBS, SLOT, 128), BF16),
            pltpu.VMEM((SUBS, SLOT, 128), BF16),
            dma((len(args),)),
            dma((3,)),
        ] + [dma((2, 2))] * 8 + [dma((SUBS,))] * 2,
        compiler_params=pltpu.CompilerParams(
            collective_id=0, has_side_effects=True, vmem_limit_bytes=60 * 1024 * 1024),
    )(*args)


def solution(mesh):
    placed = (
        P("sub", "blk", None),
        P("sub", "blk"),
        P("sub", "blk"),
        P("sub", "blk"),
        P("sub", "blk"),
        P("sub", None, "blk"),
        P("sub", None, "blk"),
        P("sub", None, "blk", None),
        P("sub", None, "blk", None),
        P("sub", None),
        P("sub", None, None),
    )
    return jax.shard_map(
        body,
        mesh=mesh,
        in_specs=placed,
        out_specs=(P("sub", "blk", None), P("sub", None, "blk", None), P("sub", "blk", None, None)),
        check_vma=False,
    )
```

```python
import jax
import jax.numpy as jnp
from jax import lax
from jax.experimental import pallas as pl
from jax.experimental.pallas import tpu as pltpu
from jax.sharding import PartitionSpec as P

MESH = pl.DeviceIdType.MESH
F32, BF16, I32 = jnp.float32, jnp.bfloat16, jnp.int32

SUBS, SIDE, PB, NB, COLS, POLES, DEPTH, STEPS = 32, 4, 64, 1024, 256, 12, 4, 2
CAP = 6
SLOT = CAP * STEPS * 2
HOPS = (1, 3, 2)
NEAR = (1,) + tuple(2 * k + c for k in (1, 15, 2, 14, 3, 13, 4, 12) for c in range(2))


def turn_tables(blk, small, table):
    port_v, far_v, delay_v, adm_v, rate_v, res_v = small
    table[...] = jnp.zeros_like(table)
    table[0:POLES, 0:PB] = rate_v[:, 0, :]
    table[16:16 + POLES, 0:PB] = res_v[:, 0, :]
    table[32:33, 0:PB] = adm_v[...]
    table[33:34, 0:PB] = far_v[...].astype(F32)
    table[34:35, 0:PB] = (port_v[...] - blk * NB).astype(F32)
    table[35:36, 0:PB] = delay_v[...].astype(F32)
    table[...] = jnp.transpose(table[...])


def advance(x, y, table, state_v, hist_v, event_v, amp_v, new_v, source, gath):
    for part in range(4):
        rows = slice(part * 16, part * 16 + 16)
        delay = table[rows, 35:36]
        arrive = []
        for step in range(STEPS):
            got = jnp.zeros((16, COLS), F32)
            for d in range(DEPTH):
                got = jnp.where(delay == float(d + step + 1), hist_v[0, d, rows, :], got)
            arrive.append(got)
        totals = [jnp.zeros((16, COLS), F32) for _ in range(STEPS)]
        for p in range(POLES):
            rate = table[rows, p:p + 1]
            weight = table[rows, 16 + p:17 + p]
            now = state_v[0, p, rows, :]
            for step in range(STEPS):
                now = rate * now + weight * arrive[step]
                totals[step] = totals[step] + now
            new_v[0, p, rows, :] = now
        index = lax.broadcasted_iota(I32, (16, COLS), 0) + ((y * SIDE + x) * PB + part * 16)
        hit = event_v[...] == index
        for step in range(STEPS):
            source[step, rows, :] = totals[step]
            kick = jnp.where(hit, amp_v[0, step:step + 1, :], 0.0)
            gath[step, y, pl.ds(pl.multiple_of(x * PB + part * 16, 16), 16), :] = (totals[step] + kick).astype(BF16)


def places(far_v, table):
    far_row = far_v[...].astype(F32)
    far_col = table[0:PB, 33:34]
    same = far_col == far_row
    ii = lax.broadcasted_iota(I32, (PB, PB), 0)
    jj = lax.broadcasted_iota(I32, (PB, PB), 1)
    rank_row = jnp.sum(jnp.where(same & (ii < jj), 1.0, 0.0), axis=0, keepdims=True)
    rank_col = jnp.sum(jnp.where(same & (jj < ii), 1.0, 0.0), axis=1, keepdims=True)
    slot_row = (far_row * SLOT + rank_row).astype(I32)
    slot_col = (far_col * SLOT + rank_col).astype(I32)
    place_row = jnp.concatenate([slot_row + q * CAP for q in range(4)], axis=1)
    place_col = jnp.concatenate([slot_col + q * CAP for q in range(4)], axis=0)
    return place_row, place_col


def masks(far_v, table, pack, unpack):
    place_row, place_col = places(far_v, table)
    pack[...] = (lax.broadcasted_iota(I32, (SUBS * SLOT, 256), 0) == place_row).astype(BF16)
    unpack[...] = (lax.broadcasted_iota(I32, (256, SUBS * SLOT), 1) == place_col).astype(BF16)


def port_rows(table, z_v, ports):
    node_col = table[0:PB, 34:35].astype(I32)
    pick = (lax.broadcasted_iota(I32, (PB, NB), 1) == node_col).astype(BF16)
    ports[...] = jnp.dot(pick, z_v[0], preferred_element_type=F32).astype(BF16)


def waves_out(table, ports, gath, source, pack, outbox):
    twice = 2.0 * table[0:PB, 32:33]
    waves = []
    for t in range(2):
        volt = jnp.dot(ports[...], gath[t].reshape(1024, COLS), preferred_element_type=F32)
        wave = (twice * volt - source[t]).astype(BF16)
        waves += [wave[:, 0:128], wave[:, 128:256]]
    stacked = jnp.concatenate(waves, axis=0)
    boxes = jnp.dot(pack[...], stacked, preferred_element_type=F32).astype(BF16)
    outbox[...] = boxes.reshape(SUBS, SLOT, 128)


def peaks(z_v, gath, peak_ref):
    for part in range(4):
        rows = slice(part * 256, part * 256 + 256)
        v0 = jnp.dot(z_v[0, rows, :], gath[0].reshape(1024, COLS), preferred_element_type=F32)
        v1 = jnp.dot(z_v[0, rows, :], gath[1].reshape(1024, COLS), preferred_element_type=F32)
        peak_ref[0, rows, :] = jnp.maximum(jnp.abs(v0), jnp.abs(v1)).astype(BF16)


def spread(unpack, inbox, arr_ref):
    got = jnp.dot(unpack[...], inbox[...].reshape(SUBS * SLOT, 128), preferred_element_type=F32)
    for t in range(2):
        arr_ref[0, :, t, 0:128] = got[128 * t:128 * t + PB]
        arr_ref[0, :, t, 128:256] = got[128 * t + PB:128 * t + 2 * PB]


def kernel(
    z_hbm, port_hbm, far_hbm, delay_hbm, adm_hbm, rate_hbm, res_hbm, state_hbm, hist_hbm, event_hbm, amp_hbm,
    peak_ref, new_ref, inbox, unpack,
    z_v, port_v, far_v, delay_v, adm_v, rate_v, res_v, state_v, hist_v, event_v, amp_v,
    table, gath, source, ports, outbox, pack,
    in_sem, ring_s, ring_r, out_sem, box_sem, met,
):
    sub = lax.axis_index("sub")
    blk = lax.axis_index("blk")
    x = lax.rem(blk, SIDE)
    y = lax.div(blk, SIDE)

    loads = []
    pairs = (
        (port_hbm, port_v), (far_hbm, far_v), (delay_hbm, delay_v), (adm_hbm, adm_v), (rate_hbm, rate_v),
        (res_hbm, res_v), (event_hbm, event_v), (amp_hbm, amp_v), (hist_hbm, hist_v), (state_hbm, state_v), (z_hbm, z_v),
    )
    for n, (src, dst) in enumerate(pairs):
        loads.append(pltpu.make_async_copy(src, dst, in_sem.at[n]))
        loads[n].start()

    def along(axis, k):
        if axis == 0:
            return y, lax.rem(x + k, SIDE)
        return lax.rem(y + k, SIDE), x

    barrier = pltpu.get_barrier_semaphore()
    for axis in range(2):
        for k in HOPS:
            py, px = along(axis, k)
            pl.semaphore_signal(barrier, inc=1, device_id=(sub, py * SIDE + px), device_id_type=MESH)

    def near(sem):
        for k in NEAR:
            z = lax.rem(lax.div(sub, 2) + k // 2, SUBS // 2)
            core = lax.rem(lax.rem(sub, 2) + k, 2)
            pl.semaphore_signal(sem, inc=1, device_id=(z * 2 + core, blk), device_id_type=MESH)

    near(barrier)

    for n in range(8):
        loads[n].wait()
    turn_tables(blk, (port_v, far_v, delay_v, adm_v, rate_v, res_v), table)
    loads[8].wait()
    loads[9].wait()
    advance(x, y, table, state_v, hist_v, event_v, amp_v, new_ref, source, gath)

    pl.semaphore_wait(barrier, 6 + len(NEAR))

    def slab(t, yy, xx, axis, k, level):
        ref = gath.at[t, yy, pl.ds(pl.multiple_of(xx * PB, 16), PB), :]
        py, px = along(axis, k)
        c = pltpu.make_async_remote_copy(
            src_ref=ref, dst_ref=ref, send_sem=ring_s.at[level, t, k], recv_sem=ring_r.at[level, t, k],
            device_id=(sub, py * SIDE + px), device_id_type=MESH)
        c.start()
        return c

    first = [[slab(t, y, x, t, k, 0) for k in HOPS] for t in range(2)]
    later = [slab(t, y, x, 1 - t, k, 1) for t in range(2) for k in HOPS]

    near(met)
    masks(far_v, table, pack, unpack)
    for n, k in enumerate(HOPS):
        for t in range(2):
            first[t][n].wait_recv()
            yy, xx = along(t, SIDE - k)
            later += [slab(t, yy, xx, 1 - t, j, 1 + k) for j in HOPS]
        if n == 0:
            loads[10].wait()
            port_rows(table, z_v, ports)
    for c in later:
        c.wait_recv()

    waves_out(table, ports, gath, source, pack, outbox)
    pl.semaphore_wait(met, len(NEAR))

    def box(k):
        d = lax.rem(sub + k, SUBS)
        return pltpu.make_async_remote_copy(
            src_ref=outbox.at[d], dst_ref=inbox.at[sub], send_sem=out_sem.at[d], recv_sem=box_sem.at[sub],
            device_id=(d, blk), device_id_type=MESH)

    def post(i, c):
        box(lax.rem(i + SUBS - sub, SUBS)).start()
        return c

    lax.fori_loop(0, sub, post, 0)
    lax.fori_loop(sub + 1, SUBS, post, 0)
    inbox[sub] = jnp.zeros((SLOT, 128), BF16)
    peaks(z_v, gath, peak_ref)

    def collect(k, c):
        d = lax.rem(sub + k, SUBS)
        pltpu.make_async_remote_copy(
            src_ref=outbox.at[d], dst_ref=inbox.at[d], send_sem=out_sem.at[d], recv_sem=box_sem.at[d],
            device_id=(d, blk), device_id_type=MESH).wait_recv()
        return c

    lax.fori_loop(1, SUBS, collect, 0)

    for c in first[0] + first[1] + later:
        c.wait_send()

    def drain(k, c):
        box(k).wait_send()
        return c

    lax.fori_loop(1, SUBS, drain, 0)


def settle(peak, new, inbox, unpack, peak_hbm, new_hbm, arr_hbm, arr, sem):
    copies = [pltpu.make_async_copy(a, b, sem.at[n]) for n, (a, b) in enumerate(((peak, peak_hbm), (new, new_hbm), (arr, arr_hbm)))]
    copies[0].start()
    copies[1].start()
    spread(unpack, inbox, arr)
    copies[2].start()
    for q in copies:
        q.wait()


HELD = (
    ((1, NB, COLS), BF16), ((1, POLES, PB, COLS), F32), ((SUBS, SLOT, 128), BF16), ((256, SUBS * SLOT), BF16),
)
OUTS = (((1, NB, COLS), BF16), ((1, POLES, PB, COLS), F32), ((1, PB, STEPS, COLS), F32))


def scratch(args):
    dma = pltpu.SemaphoreType.DMA
    return [pltpu.VMEM(a.shape, a.dtype) for a in args] + [
        pltpu.VMEM((128, 128), F32),
        pltpu.VMEM((2, SIDE, SIDE * PB, COLS), BF16),
        pltpu.VMEM((2, PB, COLS), F32),
        pltpu.VMEM((PB, 1024), BF16),
        pltpu.VMEM((SUBS, SLOT, 128), BF16),
        pltpu.VMEM((SUBS * SLOT, 256), BF16),
        dma((len(args),)),
        dma((5, 2, 4)),
        dma((5, 2, 4)),
        dma((SUBS,)),
        dma((SUBS,)),
        pltpu.SemaphoreType.REGULAR,
    ]


def body(*args):
    args = list(args)
    for n in (5, 6):
        args[n] = args[n].reshape(POLES, 1, PB)
    args = [pltpu.with_memory_space_constraint(a, pltpu.HBM) for a in args]
    held = pl.pallas_call(
        kernel,
        out_shape=[pltpu.VMEM(s, d) for s, d in HELD],
        in_specs=[pl.BlockSpec(memory_space=pltpu.HBM)] * len(args),
        out_specs=[pl.BlockSpec(memory_space=pltpu.VMEM)] * 4,
        scratch_shapes=scratch(args),
        compiler_params=pltpu.CompilerParams(
            collective_id=0, has_side_effects=True, vmem_limit_bytes=32 * 1024 * 1024),
    )(*args)
    held = [pltpu.with_memory_space_constraint(a, pltpu.VMEM) for a in held]
    return pl.pallas_call(
        settle,
        out_shape=[pltpu.HBM(s, d) for s, d in OUTS],
        in_specs=[pl.BlockSpec(memory_space=pltpu.VMEM)] * 4,
        out_specs=[pl.BlockSpec(memory_space=pltpu.HBM)] * 3,
        scratch_shapes=[pltpu.VMEM(*OUTS[2]), pltpu.SemaphoreType.DMA((3,))],
    )(*held)


def solution(mesh):
    placed = (
        P("sub", "blk", None),
        P("sub", "blk"),
        P("sub", "blk"),
        P("sub", "blk"),
        P("sub", "blk"),
        P("sub", None, "blk"),
        P("sub", None, "blk"),
        P("sub", None, "blk", None),
        P("sub", None, "blk", None),
        P("sub", None),
        P("sub", None, None),
    )
    return jax.shard_map(
        body,
        mesh=mesh,
        in_specs=placed,
        out_specs=(P("sub", "blk", None), P("sub", None, "blk", None), P("sub", "blk", None, None)),
        check_vma=False,
    )
```

```python
import jax
import jax.numpy as jnp
from jax import lax
from jax.experimental import pallas as pl
from jax.experimental.pallas import tpu as pltpu
from jax.sharding import PartitionSpec as P

MESH = pl.DeviceIdType.MESH
F32, BF16, I32 = jnp.float32, jnp.bfloat16, jnp.int32

SUBS, SIDE, PB, NB, COLS, POLES, DEPTH, STEPS = 32, 4, 64, 1024, 256, 12, 4, 2
CAP = 6
SLOT = CAP * STEPS * 2
HOPS = (1, 3, 2)
NEAR = ((0, 1),) + tuple((k, c) for k in (1, 15, 2, 14) for c in range(2))
WIDE = ((4, 0), (12, 0))


def turn_tables(blk, small, table):
    port_v, far_v, delay_v, adm_v, rate_v, res_v = small
    table[...] = jnp.zeros_like(table)
    table[0:POLES, 0:PB] = rate_v[:, 0, :]
    table[16:16 + POLES, 0:PB] = res_v[:, 0, :]
    table[32:33, 0:PB] = adm_v[...]
    table[33:34, 0:PB] = far_v[...].astype(F32)
    table[34:35, 0:PB] = (port_v[...] - blk * NB).astype(F32)
    table[35:36, 0:PB] = delay_v[...].astype(F32)
    table[...] = jnp.transpose(table[...])


def advance(x, y, table, state_v, hist_v, event_v, amp_v, new_v, source, gath):
    for part in range(4):
        rows = slice(part * 16, part * 16 + 16)
        delay = table[rows, 35:36]
        arrive = []
        for step in range(STEPS):
            got = jnp.zeros((16, COLS), F32)
            for d in range(DEPTH):
                got = jnp.where(delay == float(d + step + 1), hist_v[0, d, rows, :], got)
            arrive.append(got)
        totals = [jnp.zeros((16, COLS), F32) for _ in range(STEPS)]
        for p in range(POLES):
            rate = table[rows, p:p + 1]
            weight = table[rows, 16 + p:17 + p]
            now = state_v[0, p, rows, :]
            for step in range(STEPS):
                now = rate * now + weight * arrive[step]
                totals[step] = totals[step] + now
            new_v[0, p, rows, :] = now
        index = lax.broadcasted_iota(I32, (16, COLS), 0) + ((y * SIDE + x) * PB + part * 16)
        hit = event_v[...] == index
        for step in range(STEPS):
            source[step, rows, :] = totals[step]
            kick = jnp.where(hit, amp_v[0, step:step + 1, :], 0.0)
            gath[step, y, pl.ds(pl.multiple_of(x * PB + part * 16, 16), 16), :] = (totals[step] + kick).astype(BF16)


def places(far_v, table):
    far_row = far_v[...].astype(F32)
    far_col = table[0:PB, 33:34]
    same = far_col == far_row
    ii = lax.broadcasted_iota(I32, (PB, PB), 0)
    jj = lax.broadcasted_iota(I32, (PB, PB), 1)
    rank_row = jnp.sum(jnp.where(same & (ii < jj), 1.0, 0.0), axis=0, keepdims=True)
    rank_col = jnp.sum(jnp.where(same & (jj < ii), 1.0, 0.0), axis=1, keepdims=True)
    slot_row = (far_row * SLOT + rank_row).astype(I32)
    slot_col = (far_col * SLOT + rank_col).astype(I32)
    place_row = jnp.concatenate([slot_row + q * CAP for q in range(4)], axis=1)
    place_col = jnp.concatenate([slot_col + q * CAP for q in range(4)], axis=0)
    return place_row, place_col


def masks(far_v, table, pack, unpack):
    place_row, place_col = places(far_v, table)
    pack[...] = (lax.broadcasted_iota(I32, (SUBS * SLOT, 256), 0) == place_row).astype(BF16)
    unpack[...] = (lax.broadcasted_iota(I32, (256, SUBS * SLOT), 1) == place_col).astype(BF16)


def port_rows(table, z_v, ports):
    node_col = table[0:PB, 34:35].astype(I32)
    pick = (lax.broadcasted_iota(I32, (PB, NB), 1) == node_col).astype(BF16)
    ports[...] = jnp.dot(pick, z_v[0], preferred_element_type=F32).astype(BF16)


def waves_out(table, ports, gath, source, pack, outbox):
    twice = 2.0 * table[0:PB, 32:33]
    waves = []
    for t in range(2):
        volt = jnp.dot(ports[...], gath[t].reshape(1024, COLS), preferred_element_type=F32)
        wave = (twice * volt - source[t]).astype(BF16)
        waves += [wave[:, 0:128], wave[:, 128:256]]
    stacked = jnp.concatenate(waves, axis=0)
    boxes = jnp.dot(pack[...], stacked, preferred_element_type=F32).astype(BF16)
    outbox[...] = boxes.reshape(SUBS, SLOT, 128)


def peaks(z_v, gath, peak_ref, part):
    for part in (part,):
        rows = slice(part * 256, part * 256 + 256)
        v0 = jnp.dot(z_v[0, rows, :], gath[0].reshape(1024, COLS), preferred_element_type=F32)
        v1 = jnp.dot(z_v[0, rows, :], gath[1].reshape(1024, COLS), preferred_element_type=F32)
        peak_ref[0, rows, :] = jnp.maximum(jnp.abs(v0), jnp.abs(v1)).astype(BF16)


def spread(unpack, inbox, arr_ref):
    got = jnp.dot(unpack[...], inbox[...].reshape(SUBS * SLOT, 128), preferred_element_type=F32)
    for t in range(2):
        arr_ref[0, :, t, 0:128] = got[128 * t:128 * t + PB]
        arr_ref[0, :, t, 128:256] = got[128 * t + PB:128 * t + 2 * PB]


def kernel(
    z_hbm, port_hbm, far_hbm, delay_hbm, adm_hbm, rate_hbm, res_hbm, state_hbm, hist_hbm, event_hbm, amp_hbm,
    peak_ref, new_ref, inbox, unpack,
    z_v, port_v, far_v, delay_v, adm_v, rate_v, res_v, state_v, hist_v, event_v, amp_v,
    table, gath, source, ports, outbox, pack,
    in_sem, ring_s, ring_r, out_sem, box_sem, met, wide,
):
    sub = lax.axis_index("sub")
    blk = lax.axis_index("blk")
    x = lax.rem(blk, SIDE)
    y = lax.div(blk, SIDE)

    loads = []
    pairs = (
        (port_hbm, port_v), (far_hbm, far_v), (delay_hbm, delay_v), (adm_hbm, adm_v), (rate_hbm, rate_v),
        (res_hbm, res_v), (event_hbm, event_v), (amp_hbm, amp_v), (hist_hbm, hist_v), (state_hbm, state_v), (z_hbm, z_v),
    )
    for n, (src, dst) in enumerate(pairs):
        loads.append(pltpu.make_async_copy(src, dst, in_sem.at[n]))
        if n < 10:
            loads[n].start()

    def along(axis, k):
        if axis == 0:
            return y, lax.rem(x + k, SIDE)
        return lax.rem(y + k, SIDE), x

    barrier = pltpu.get_barrier_semaphore()
    for axis in range(2):
        for k in HOPS:
            py, px = along(axis, k)
            pl.semaphore_signal(barrier, inc=1, device_id=(sub, py * SIDE + px), device_id_type=MESH)

    chip, core = lax.div(sub, 2), lax.rem(sub, 2)

    def tell(sem, offsets):
        for k, c in offsets:
            peer = lax.rem(chip + k, SUBS // 2) * 2 + lax.rem(core + c, 2)
            pl.semaphore_signal(sem, inc=1, device_id=(peer, blk), device_id_type=MESH)

    tell(barrier, NEAR)

    for n in range(8):
        loads[n].wait()
    turn_tables(blk, (port_v, far_v, delay_v, adm_v, rate_v, res_v), table)
    loads[8].wait()
    loads[9].wait()
    loads[10].start()
    advance(x, y, table, state_v, hist_v, event_v, amp_v, new_ref, source, gath)

    pl.semaphore_wait(barrier, 6 + len(NEAR))

    def slab(t, yy, xx, axis, k, level):
        ref = gath.at[t, yy, pl.ds(pl.multiple_of(xx * PB, 16), PB), :]
        py, px = along(axis, k)
        c = pltpu.make_async_remote_copy(
            src_ref=ref, dst_ref=ref, send_sem=ring_s.at[level, t, k], recv_sem=ring_r.at[level, t, k],
            device_id=(sub, py * SIDE + px), device_id_type=MESH)
        c.start()
        return c

    first = [[slab(t, y, x, t, k, 0) for k in HOPS] for t in range(2)]
    later = [slab(t, y, x, 1 - t, k, 1) for t in range(2) for k in HOPS]

    tell(met, NEAR)
    masks(far_v, table, pack, unpack)
    for n, k in enumerate(HOPS):
        for t in range(2):
            first[t][n].wait_recv()
            yy, xx = along(t, SIDE - k)
            later += [slab(t, yy, xx, 1 - t, j, 1 + k) for j in HOPS]
        if n == 0:
            pl.semaphore_wait(met, len(NEAR))
            tell(wide, WIDE)
            loads[10].wait()
            port_rows(table, z_v, ports)
    for c in later:
        c.wait_recv()

    waves_out(table, ports, gath, source, pack, outbox)
    pl.semaphore_wait(wide, len(WIDE))

    def box(k):
        d = lax.rem(sub + k, SUBS)
        return pltpu.make_async_remote_copy(
            src_ref=outbox.at[d], dst_ref=inbox.at[sub], send_sem=out_sem.at[d], recv_sem=box_sem.at[sub],
            device_id=(d, blk), device_id_type=MESH)

    def post(i, c):
        box(lax.rem(i + SUBS - sub, SUBS)).start()
        return c

    for part in range(4):
        lo = part * 8
        lax.fori_loop(lo, jnp.clip(sub, lo, lo + 8), post, 0)
        lax.fori_loop(jnp.clip(sub + 1, lo, lo + 8), lo + 8, post, 0)
        peaks(z_v, gath, peak_ref, part)
    inbox[sub] = jnp.zeros((SLOT, 128), BF16)

    def collect(k, c):
        d = lax.rem(sub + k, SUBS)
        pltpu.make_async_remote_copy(
            src_ref=outbox.at[d], dst_ref=inbox.at[d], send_sem=out_sem.at[d], recv_sem=box_sem.at[d],
            device_id=(d, blk), device_id_type=MESH).wait_recv()
        return c

    lax.fori_loop(1, SUBS, collect, 0)

    for c in first[0] + first[1] + later:
        c.wait_send()

    def drain(k, c):
        box(k).wait_send()
        return c

    lax.fori_loop(1, SUBS, drain, 0)


def settle(peak, new, inbox, unpack, peak_hbm, new_hbm, arr_hbm, arr, sem):
    copies = [pltpu.make_async_copy(a, b, sem.at[n]) for n, (a, b) in enumerate(((peak, peak_hbm), (new, new_hbm), (arr, arr_hbm)))]
    copies[0].start()
    copies[1].start()
    spread(unpack, inbox, arr)
    copies[2].start()
    for q in copies:
        q.wait()


HELD = (
    ((1, NB, COLS), BF16), ((1, POLES, PB, COLS), F32), ((SUBS, SLOT, 128), BF16), ((256, SUBS * SLOT), BF16),
)
OUTS = (((1, NB, COLS), BF16), ((1, POLES, PB, COLS), F32), ((1, PB, STEPS, COLS), F32))


def scratch(args):
    dma = pltpu.SemaphoreType.DMA
    return [pltpu.VMEM(a.shape, a.dtype) for a in args] + [
        pltpu.VMEM((128, 128), F32),
        pltpu.VMEM((2, SIDE, SIDE * PB, COLS), BF16),
        pltpu.VMEM((2, PB, COLS), F32),
        pltpu.VMEM((PB, 1024), BF16),
        pltpu.VMEM((SUBS, SLOT, 128), BF16),
        pltpu.VMEM((SUBS * SLOT, 256), BF16),
        dma((len(args),)),
        dma((5, 2, 4)),
        dma((5, 2, 4)),
        dma((SUBS,)),
        dma((SUBS,)),
        pltpu.SemaphoreType.REGULAR,
        pltpu.SemaphoreType.REGULAR,
    ]


def body(*args):
    args = list(args)
    for n in (5, 6):
        args[n] = args[n].reshape(POLES, 1, PB)
    args = [pltpu.with_memory_space_constraint(a, pltpu.HBM) for a in args]
    held = pl.pallas_call(
        kernel,
        out_shape=[pltpu.VMEM(s, d) for s, d in HELD],
        in_specs=[pl.BlockSpec(memory_space=pltpu.HBM)] * len(args),
        out_specs=[pl.BlockSpec(memory_space=pltpu.VMEM)] * 4,
        scratch_shapes=scratch(args),
        compiler_params=pltpu.CompilerParams(
            collective_id=0, has_side_effects=True, vmem_limit_bytes=32 * 1024 * 1024),
    )(*args)
    held = [pltpu.with_memory_space_constraint(a, pltpu.VMEM) for a in held]
    return pl.pallas_call(
        settle,
        out_shape=[pltpu.HBM(s, d) for s, d in OUTS],
        in_specs=[pl.BlockSpec(memory_space=pltpu.VMEM)] * 4,
        out_specs=[pl.BlockSpec(memory_space=pltpu.HBM)] * 3,
        scratch_shapes=[pltpu.VMEM(*OUTS[2]), pltpu.SemaphoreType.DMA((3,))],
    )(*held)


def solution(mesh):
    placed = (
        P("sub", "blk", None),
        P("sub", "blk"),
        P("sub", "blk"),
        P("sub", "blk"),
        P("sub", "blk"),
        P("sub", None, "blk"),
        P("sub", None, "blk"),
        P("sub", None, "blk", None),
        P("sub", None, "blk", None),
        P("sub", None),
        P("sub", None, None),
    )
    return jax.shard_map(
        body,
        mesh=mesh,
        in_specs=placed,
        out_specs=(P("sub", "blk", None), P("sub", None, "blk", None), P("sub", "blk", None, None)),
        check_vma=False,
    )
```

```python
import jax
import jax.numpy as jnp
from jax import lax
from jax.experimental import pallas as pl
from jax.experimental.pallas import tpu as pltpu
from jax.sharding import PartitionSpec as P

MESH = pl.DeviceIdType.MESH
F32, BF16, I32 = jnp.float32, jnp.bfloat16, jnp.int32

SUBS, SIDE, PB, NB, COLS, POLES, DEPTH, STEPS = 32, 4, 64, 1024, 256, 12, 4, 2
CAP = 6
SLOT = CAP * STEPS * 2
HOPS = (1, 3, 2)
NEAR = ((0, 1),) + tuple((k, c) for k in (1, 15, 2, 14) for c in range(2))
WIDE = ((4, 0), (12, 0))


def turn_tables(blk, small, table):
    port_v, far_v, delay_v, adm_v, rate_v, res_v = small
    table[...] = jnp.zeros_like(table)
    table[0:POLES, 0:PB] = rate_v[:, 0, :]
    table[16:16 + POLES, 0:PB] = res_v[:, 0, :]
    table[32:33, 0:PB] = adm_v[...]
    table[33:34, 0:PB] = far_v[...].astype(F32)
    table[34:35, 0:PB] = (port_v[...] - blk * NB).astype(F32)
    table[35:36, 0:PB] = delay_v[...].astype(F32)
    table[...] = jnp.transpose(table[...])


def advance(x, y, table, state_v, hist_v, event_v, amp_v, new_v, source, gath):
    for part in range(4):
        rows = slice(part * 16, part * 16 + 16)
        delay = table[rows, 35:36]
        arrive = []
        for step in range(STEPS):
            got = jnp.zeros((16, COLS), F32)
            for d in range(DEPTH):
                got = jnp.where(delay == float(d + step + 1), hist_v[0, d, rows, :], got)
            arrive.append(got)
        totals = [jnp.zeros((16, COLS), F32) for _ in range(STEPS)]
        for p in range(POLES):
            rate = table[rows, p:p + 1]
            weight = table[rows, 16 + p:17 + p]
            now = state_v[0, p, rows, :]
            for step in range(STEPS):
                now = rate * now + weight * arrive[step]
                totals[step] = totals[step] + now
            new_v[0, p, rows, :] = now
        index = lax.broadcasted_iota(I32, (16, COLS), 0) + ((y * SIDE + x) * PB + part * 16)
        hit = event_v[...] == index
        for step in range(STEPS):
            source[step, rows, :] = totals[step]
            kick = jnp.where(hit, amp_v[0, step:step + 1, :], 0.0)
            gath[step, y, pl.ds(pl.multiple_of(x * PB + part * 16, 16), 16), :] = (totals[step] + kick).astype(BF16)


def places(far_v, table):
    far_row = far_v[...].astype(F32)
    far_col = table[0:PB, 33:34]
    same = far_col == far_row
    ii = lax.broadcasted_iota(I32, (PB, PB), 0)
    jj = lax.broadcasted_iota(I32, (PB, PB), 1)
    rank_row = jnp.sum(jnp.where(same & (ii < jj), 1.0, 0.0), axis=0, keepdims=True)
    rank_col = jnp.sum(jnp.where(same & (jj < ii), 1.0, 0.0), axis=1, keepdims=True)
    slot_row = (far_row * SLOT + rank_row).astype(I32)
    slot_col = (far_col * SLOT + rank_col).astype(I32)
    place_row = jnp.concatenate([slot_row + q * CAP for q in range(4)], axis=1)
    place_col = jnp.concatenate([slot_col + q * CAP for q in range(4)], axis=0)
    return place_row, place_col


def masks(far_v, table, pack, unpack):
    place_row, place_col = places(far_v, table)
    pack[...] = (lax.broadcasted_iota(I32, (SUBS * SLOT, 256), 0) == place_row).astype(BF16)
    unpack[...] = (lax.broadcasted_iota(I32, (256, SUBS * SLOT), 1) == place_col).astype(BF16)


def port_rows(table, z_v, ports):
    node_col = table[0:PB, 34:35].astype(I32)
    pick = (lax.broadcasted_iota(I32, (PB, NB), 1) == node_col).astype(BF16)
    ports[...] = jnp.dot(pick, z_v[0], preferred_element_type=F32).astype(BF16)


def waves_out(table, ports, gath, source, pack, outbox):
    twice = 2.0 * table[0:PB, 32:33]
    waves = []
    for t in range(2):
        volt = jnp.dot(ports[...], gath[t].reshape(1024, COLS), preferred_element_type=F32)
        wave = (twice * volt - source[t]).astype(BF16)
        waves += [wave[:, 0:128], wave[:, 128:256]]
    stacked = jnp.concatenate(waves, axis=0)
    boxes = jnp.dot(pack[...], stacked, preferred_element_type=F32).astype(BF16)
    outbox[...] = boxes.reshape(SUBS, SLOT, 128)


def peaks(z_v, gath, peak_ref, part):
    for part in (part,):
        rows = slice(part * 256, part * 256 + 256)
        v0 = jnp.dot(z_v[0, rows, :], gath[0].reshape(1024, COLS), preferred_element_type=F32)
        v1 = jnp.dot(z_v[0, rows, :], gath[1].reshape(1024, COLS), preferred_element_type=F32)
        peak_ref[0, rows, :] = jnp.maximum(jnp.abs(v0), jnp.abs(v1)).astype(BF16)


def spread(unpack, inbox, arr_ref):
    got = jnp.dot(unpack[...], inbox[...].reshape(SUBS * SLOT, 128), preferred_element_type=F32)
    for t in range(2):
        arr_ref[0, :, t, 0:128] = got[128 * t:128 * t + PB]
        arr_ref[0, :, t, 128:256] = got[128 * t + PB:128 * t + 2 * PB]


def kernel(
    z_hbm, port_hbm, far_hbm, delay_hbm, adm_hbm, rate_hbm, res_hbm, state_hbm, hist_hbm, event_hbm, amp_hbm,
    peak_ref, new_ref, inbox, unpack,
    z_v, port_v, far_v, delay_v, adm_v, rate_v, res_v, state_v, hist_v, event_v, amp_v,
    table, gath, source, ports, outbox, pack,
    in_sem, ring_s, ring_r, out_sem, box_sem, met, wide,
):
    sub = lax.axis_index("sub")
    blk = lax.axis_index("blk")
    x = lax.rem(blk, SIDE)
    y = lax.div(blk, SIDE)

    loads = []
    pairs = (
        (port_hbm, port_v), (far_hbm, far_v), (delay_hbm, delay_v), (adm_hbm, adm_v), (rate_hbm, rate_v),
        (res_hbm, res_v), (event_hbm, event_v), (amp_hbm, amp_v), (hist_hbm, hist_v), (state_hbm, state_v), (z_hbm, z_v),
    )
    for n, (src, dst) in enumerate(pairs):
        loads.append(pltpu.make_async_copy(src, dst, in_sem.at[n]))
        if n < 10:
            loads[n].start()

    def along(axis, k):
        if axis == 0:
            return y, lax.rem(x + k, SIDE)
        return lax.rem(y + k, SIDE), x

    barrier = pltpu.get_barrier_semaphore()
    for axis in range(2):
        for k in HOPS:
            py, px = along(axis, k)
            pl.semaphore_signal(barrier, inc=1, device_id=(sub, py * SIDE + px), device_id_type=MESH)

    chip, core = lax.div(sub, 2), lax.rem(sub, 2)

    def tell(sem, offsets):
        for k, c in offsets:
            peer = lax.rem(chip + k, SUBS // 2) * 2 + lax.rem(core + c, 2)
            pl.semaphore_signal(sem, inc=1, device_id=(peer, blk), device_id_type=MESH)

    tell(barrier, NEAR)

    for n in range(8):
        loads[n].wait()
    turn_tables(blk, (port_v, far_v, delay_v, adm_v, rate_v, res_v), table)
    loads[8].wait()
    loads[9].wait()
    loads[10].start()
    advance(x, y, table, state_v, hist_v, event_v, amp_v, new_ref, source, gath)

    pl.semaphore_wait(barrier, 6 + len(NEAR))

    def slab(t, yy, xx, axis, k, level):
        ref = gath.at[t, yy, pl.ds(pl.multiple_of(xx * PB, 16), PB), :]
        py, px = along(axis, k)
        c = pltpu.make_async_remote_copy(
            src_ref=ref, dst_ref=ref, send_sem=ring_s.at[level, t, k], recv_sem=ring_r.at[level, t, k],
            device_id=(sub, py * SIDE + px), device_id_type=MESH)
        c.start()
        return c

    first = [[slab(t, y, x, t, k, 0) for k in HOPS] for t in range(2)]
    later = [slab(t, y, x, 1 - t, k, 1) for t in range(2) for k in HOPS]

    tell(met, NEAR)
    masks(far_v, table, pack, unpack)
    for n, k in enumerate(HOPS):
        for t in range(2):
            first[t][n].wait_recv()
            yy, xx = along(t, SIDE - k)
            later += [slab(t, yy, xx, 1 - t, j, 1 + k) for j in HOPS]
        if n == 0:
            pl.semaphore_wait(met, len(NEAR))
            tell(wide, WIDE)
            loads[10].wait()
            port_rows(table, z_v, ports)
    for c in later:
        c.wait_recv()

    waves_out(table, ports, gath, source, pack, outbox)
    pl.semaphore_wait(wide, len(WIDE))

    def box(k):
        d = lax.rem(sub + k, SUBS)
        return pltpu.make_async_remote_copy(
            src_ref=outbox.at[d], dst_ref=inbox.at[sub], send_sem=out_sem.at[d], recv_sem=box_sem.at[sub],
            device_id=(d, blk), device_id_type=MESH)

    def post(i, c):
        box(lax.rem(i + SUBS - sub, SUBS)).start()
        return c

    for part in range(4):
        lo = part * 8
        lax.fori_loop(lo, jnp.clip(sub, lo, lo + 8), post, 0)
        lax.fori_loop(jnp.clip(sub + 1, lo, lo + 8), lo + 8, post, 0)
        peaks(z_v, gath, peak_ref, part)
    inbox[sub] = jnp.zeros((SLOT, 128), BF16)

    for c in first[0] + first[1] + later:
        c.wait_send()

    def drain(k, c):
        box(k).wait_send()
        return c

    lax.fori_loop(1, SUBS, drain, 0)

    def arrived(d):
        pltpu.make_async_remote_copy(
            src_ref=outbox.at[d], dst_ref=inbox.at[d], send_sem=out_sem.at[d], recv_sem=box_sem.at[d],
            device_id=(d, blk), device_id_type=MESH).wait_recv()

    arrived(chip * 2 + 1 - core)

    def collect(k, c):
        for far in (k, SUBS // 2 - k):
            for side in range(2):
                arrived(lax.rem(chip + far, SUBS // 2) * 2 + side)
        return c

    lax.fori_loop(1, SUBS // 4, collect, 0)
    for side in range(2):
        arrived(lax.rem(chip + SUBS // 4, SUBS // 2) * 2 + side)


def settle(peak, new, inbox, unpack, peak_hbm, new_hbm, arr_hbm, arr, sem):
    copies = [pltpu.make_async_copy(a, b, sem.at[n]) for n, (a, b) in enumerate(((peak, peak_hbm), (new, new_hbm), (arr, arr_hbm)))]
    copies[0].start()
    copies[1].start()
    spread(unpack, inbox, arr)
    copies[2].start()
    for q in copies:
        q.wait()


HELD = (
    ((1, NB, COLS), BF16), ((1, POLES, PB, COLS), F32), ((SUBS, SLOT, 128), BF16), ((256, SUBS * SLOT), BF16),
)
OUTS = (((1, NB, COLS), BF16), ((1, POLES, PB, COLS), F32), ((1, PB, STEPS, COLS), F32))


def scratch(args):
    dma = pltpu.SemaphoreType.DMA
    return [pltpu.VMEM(a.shape, a.dtype) for a in args] + [
        pltpu.VMEM((128, 128), F32),
        pltpu.VMEM((2, SIDE, SIDE * PB, COLS), BF16),
        pltpu.VMEM((2, PB, COLS), F32),
        pltpu.VMEM((PB, 1024), BF16),
        pltpu.VMEM((SUBS, SLOT, 128), BF16),
        pltpu.VMEM((SUBS * SLOT, 256), BF16),
        dma((len(args),)),
        dma((5, 2, 4)),
        dma((5, 2, 4)),
        dma((SUBS,)),
        dma((SUBS,)),
        pltpu.SemaphoreType.REGULAR,
        pltpu.SemaphoreType.REGULAR,
    ]


def body(*args):
    args = list(args)
    for n in (5, 6):
        args[n] = args[n].reshape(POLES, 1, PB)
    args = [pltpu.with_memory_space_constraint(a, pltpu.HBM) for a in args]
    held = pl.pallas_call(
        kernel,
        out_shape=[pltpu.VMEM(s, d) for s, d in HELD],
        in_specs=[pl.BlockSpec(memory_space=pltpu.HBM)] * len(args),
        out_specs=[pl.BlockSpec(memory_space=pltpu.VMEM)] * 4,
        scratch_shapes=scratch(args),
        compiler_params=pltpu.CompilerParams(
            collective_id=0, has_side_effects=True, vmem_limit_bytes=32 * 1024 * 1024),
    )(*args)
    held = [pltpu.with_memory_space_constraint(a, pltpu.VMEM) for a in held]
    return pl.pallas_call(
        settle,
        out_shape=[pltpu.HBM(s, d) for s, d in OUTS],
        in_specs=[pl.BlockSpec(memory_space=pltpu.VMEM)] * 4,
        out_specs=[pl.BlockSpec(memory_space=pltpu.HBM)] * 3,
        scratch_shapes=[pltpu.VMEM(*OUTS[2]), pltpu.SemaphoreType.DMA((3,))],
    )(*held)


def solution(mesh):
    placed = (
        P("sub", "blk", None),
        P("sub", "blk"),
        P("sub", "blk"),
        P("sub", "blk"),
        P("sub", "blk"),
        P("sub", None, "blk"),
        P("sub", None, "blk"),
        P("sub", None, "blk", None),
        P("sub", None, "blk", None),
        P("sub", None),
        P("sub", None, None),
    )
    return jax.shard_map(
        body,
        mesh=mesh,
        in_specs=placed,
        out_specs=(P("sub", "blk", None), P("sub", None, "blk", None), P("sub", "blk", None, None)),
        check_vma=False,
    )
```

```python
import jax
import jax.numpy as jnp
from jax import lax
from jax.experimental import pallas as pl
from jax.experimental.pallas import tpu as pltpu
from jax.sharding import PartitionSpec as P

MESH = pl.DeviceIdType.MESH
F32, BF16, I32 = jnp.float32, jnp.bfloat16, jnp.int32

SUBS, SIDE, PB, NB, COLS, POLES, DEPTH, STEPS = 32, 4, 64, 1024, 256, 12, 4, 2
CAP = 6
SLOT = CAP * STEPS * 2
HOPS = (1, 3, 2)
NEAR = ((0, 1),) + tuple((k, c) for k in (1, 15, 2, 14) for c in range(2))
WIDE = ((4, 0), (12, 0))


def turn_tables(blk, small, table):
    port_v, far_v, delay_v, adm_v, rate_v, res_v = small
    table[...] = jnp.zeros_like(table)
    table[0:POLES, 0:PB] = rate_v[:, 0, :]
    table[16:16 + POLES, 0:PB] = res_v[:, 0, :]
    table[32:33, 0:PB] = adm_v[...]
    table[33:34, 0:PB] = far_v[...].astype(F32)
    table[34:35, 0:PB] = (port_v[...] - blk * NB).astype(F32)
    table[35:36, 0:PB] = delay_v[...].astype(F32)
    table[...] = jnp.transpose(table[...])


def advance(x, y, table, state_v, hist_v, event_v, amp_v, new_v, source, gath):
    for part in range(4):
        rows = slice(part * 16, part * 16 + 16)
        delay = table[rows, 35:36]
        arrive = []
        for step in range(STEPS):
            got = jnp.zeros((16, COLS), F32)
            for d in range(DEPTH):
                got = jnp.where(delay == float(d + step + 1), hist_v[0, d, rows, :], got)
            arrive.append(got)
        totals = [jnp.zeros((16, COLS), F32) for _ in range(STEPS)]
        for p in range(POLES):
            rate = table[rows, p:p + 1]
            weight = table[rows, 16 + p:17 + p]
            now = state_v[0, p, rows, :]
            for step in range(STEPS):
                now = rate * now + weight * arrive[step]
                totals[step] = totals[step] + now
            new_v[0, p, rows, :] = now
        index = lax.broadcasted_iota(I32, (16, COLS), 0) + ((y * SIDE + x) * PB + part * 16)
        hit = event_v[...] == index
        for step in range(STEPS):
            source[step, rows, :] = totals[step]
            kick = jnp.where(hit, amp_v[0, step:step + 1, :], 0.0)
            gath[step, y, pl.ds(pl.multiple_of(x * PB + part * 16, 16), 16), :] = (totals[step] + kick).astype(BF16)


def places(far_v, table):
    far_row = far_v[...].astype(F32)
    far_col = table[0:PB, 33:34]
    same = far_col == far_row
    ii = lax.broadcasted_iota(I32, (PB, PB), 0)
    jj = lax.broadcasted_iota(I32, (PB, PB), 1)
    rank_row = jnp.sum(jnp.where(same & (ii < jj), 1.0, 0.0), axis=0, keepdims=True)
    rank_col = jnp.sum(jnp.where(same & (jj < ii), 1.0, 0.0), axis=1, keepdims=True)
    slot_row = (far_row * SLOT + rank_row).astype(I32)
    slot_col = (far_col * SLOT + rank_col).astype(I32)
    place_row = jnp.concatenate([slot_row + q * CAP for q in range(4)], axis=1)
    place_col = jnp.concatenate([slot_col + q * CAP for q in range(4)], axis=0)
    return place_row, place_col


def masks(far_v, table, pack, unpack):
    place_row, place_col = places(far_v, table)
    pack[...] = (lax.broadcasted_iota(I32, (SUBS * SLOT, 256), 0) == place_row).astype(BF16)
    unpack[...] = (lax.broadcasted_iota(I32, (256, SUBS * SLOT), 1) == place_col).astype(BF16)


def port_rows(table, z_v, ports):
    node_col = table[0:PB, 34:35].astype(I32)
    pick = (lax.broadcasted_iota(I32, (PB, NB), 1) == node_col).astype(BF16)
    ports[...] = jnp.dot(pick, z_v[0], preferred_element_type=F32).astype(BF16)


def waves_out(table, ports, gath, source):
    twice = 2.0 * table[0:PB, 32:33]
    waves = []
    for t in range(2):
        volt = jnp.dot(ports[...], gath[t].reshape(1024, COLS), preferred_element_type=F32)
        wave = (twice * volt - source[t]).astype(BF16)
        waves += [wave[:, 0:128], wave[:, 128:256]]
    return jnp.concatenate(waves, axis=0)


def fill(part, waves, pack, outbox):
    rows = slice(part * 8 * SLOT, part * 8 * SLOT + 8 * SLOT)
    boxes = jnp.dot(pack[rows, :], waves, preferred_element_type=F32).astype(BF16)
    outbox[part * 8:part * 8 + 8] = boxes.reshape(8, SLOT, 128)


def peaks(z_v, gath, peak_ref, part):
    for part in (part,):
        rows = slice(part * 256, part * 256 + 256)
        v0 = jnp.dot(z_v[0, rows, :], gath[0].reshape(1024, COLS), preferred_element_type=F32)
        v1 = jnp.dot(z_v[0, rows, :], gath[1].reshape(1024, COLS), preferred_element_type=F32)
        peak_ref[0, rows, :] = jnp.maximum(jnp.abs(v0), jnp.abs(v1)).astype(BF16)


def spread(unpack, inbox, arr_ref):
    got = jnp.dot(unpack[...], inbox[...].reshape(SUBS * SLOT, 128), preferred_element_type=F32)
    for t in range(2):
        arr_ref[0, :, t, 0:128] = got[128 * t:128 * t + PB]
        arr_ref[0, :, t, 128:256] = got[128 * t + PB:128 * t + 2 * PB]


def kernel(
    z_hbm, port_hbm, far_hbm, delay_hbm, adm_hbm, rate_hbm, res_hbm, state_hbm, hist_hbm, event_hbm, amp_hbm,
    peak_ref, new_ref, inbox, unpack,
    z_v, port_v, far_v, delay_v, adm_v, rate_v, res_v, state_v, hist_v, event_v, amp_v,
    table, gath, source, ports, outbox, pack,
    in_sem, ring_s, ring_r, out_sem, box_sem, met, wide,
):
    sub = lax.axis_index("sub")
    blk = lax.axis_index("blk")
    x = lax.rem(blk, SIDE)
    y = lax.div(blk, SIDE)

    loads = []
    pairs = (
        (port_hbm, port_v), (far_hbm, far_v), (delay_hbm, delay_v), (adm_hbm, adm_v), (rate_hbm, rate_v),
        (res_hbm, res_v), (event_hbm, event_v), (amp_hbm, amp_v), (hist_hbm, hist_v), (state_hbm, state_v), (z_hbm, z_v),
    )
    for n, (src, dst) in enumerate(pairs):
        loads.append(pltpu.make_async_copy(src, dst, in_sem.at[n]))
        if n < 10:
            loads[n].start()

    def along(axis, k):
        if axis == 0:
            return y, lax.rem(x + k, SIDE)
        return lax.rem(y + k, SIDE), x

    barrier = pltpu.get_barrier_semaphore()
    for axis in range(2):
        for k in HOPS:
            py, px = along(axis, k)
            pl.semaphore_signal(barrier, inc=1, device_id=(sub, py * SIDE + px), device_id_type=MESH)

    chip, core = lax.div(sub, 2), lax.rem(sub, 2)

    def tell(sem, offsets):
        for k, c in offsets:
            peer = lax.rem(chip + k, SUBS // 2) * 2 + lax.rem(core + c, 2)
            pl.semaphore_signal(sem, inc=1, device_id=(peer, blk), device_id_type=MESH)

    tell(barrier, NEAR)

    for n in range(8):
        loads[n].wait()
    turn_tables(blk, (port_v, far_v, delay_v, adm_v, rate_v, res_v), table)
    loads[8].wait()
    loads[9].wait()
    loads[10].start()
    advance(x, y, table, state_v, hist_v, event_v, amp_v, new_ref, source, gath)

    pl.semaphore_wait(barrier, 6 + len(NEAR))

    def slab(t, yy, xx, axis, k, level):
        ref = gath.at[t, yy, pl.ds(pl.multiple_of(xx * PB, 16), PB), :]
        py, px = along(axis, k)
        c = pltpu.make_async_remote_copy(
            src_ref=ref, dst_ref=ref, send_sem=ring_s.at[level, t, k], recv_sem=ring_r.at[level, t, k],
            device_id=(sub, py * SIDE + px), device_id_type=MESH)
        c.start()
        return c

    first = [[slab(t, y, x, t, k, 0) for k in HOPS] for t in range(2)]
    later = [slab(t, y, x, 1 - t, k, 1) for t in range(2) for k in HOPS]

    tell(met, NEAR)
    masks(far_v, table, pack, unpack)
    for n, k in enumerate(HOPS):
        for t in range(2):
            first[t][n].wait_recv()
            yy, xx = along(t, SIDE - k)
            later += [slab(t, yy, xx, 1 - t, j, 1 + k) for j in HOPS]
        if n == 0:
            pl.semaphore_wait(met, len(NEAR))
            tell(wide, WIDE)
            loads[10].wait()
            port_rows(table, z_v, ports)
    for c in later:
        c.wait_recv()

    waves = waves_out(table, ports, gath, source)
    pl.semaphore_wait(wide, len(WIDE))

    def box(k):
        d = lax.rem(sub + k, SUBS)
        return pltpu.make_async_remote_copy(
            src_ref=outbox.at[d], dst_ref=inbox.at[sub], send_sem=out_sem.at[d], recv_sem=box_sem.at[sub],
            device_id=(d, blk), device_id_type=MESH)

    def post(i, c):
        box(lax.rem(i + SUBS - sub, SUBS)).start()
        return c

    for part in range(4):
        lo = part * 8
        fill(part, waves, pack, outbox)
        lax.fori_loop(lo, jnp.clip(sub, lo, lo + 8), post, 0)
        lax.fori_loop(jnp.clip(sub + 1, lo, lo + 8), lo + 8, post, 0)
        peaks(z_v, gath, peak_ref, part)
    inbox[sub] = jnp.zeros((SLOT, 128), BF16)

    for c in first[0] + first[1] + later:
        c.wait_send()

    def drain(k, c):
        box(k).wait_send()
        return c

    lax.fori_loop(1, SUBS, drain, 0)

    def arrived(d):
        pltpu.make_async_remote_copy(
            src_ref=outbox.at[d], dst_ref=inbox.at[d], send_sem=out_sem.at[d], recv_sem=box_sem.at[d],
            device_id=(d, blk), device_id_type=MESH).wait_recv()

    arrived(chip * 2 + 1 - core)

    def collect(k, c):
        for far in (k, SUBS // 2 - k):
            for side in range(2):
                arrived(lax.rem(chip + far, SUBS // 2) * 2 + side)
        return c

    lax.fori_loop(1, SUBS // 4, collect, 0)
    for side in range(2):
        arrived(lax.rem(chip + SUBS // 4, SUBS // 2) * 2 + side)


def settle(peak, new, inbox, unpack, peak_hbm, new_hbm, arr_hbm, arr, sem):
    copies = [pltpu.make_async_copy(a, b, sem.at[n]) for n, (a, b) in enumerate(((peak, peak_hbm), (new, new_hbm), (arr, arr_hbm)))]
    copies[0].start()
    copies[1].start()
    spread(unpack, inbox, arr)
    copies[2].start()
    for q in copies:
        q.wait()


HELD = (
    ((1, NB, COLS), BF16), ((1, POLES, PB, COLS), F32), ((SUBS, SLOT, 128), BF16), ((256, SUBS * SLOT), BF16),
)
OUTS = (((1, NB, COLS), BF16), ((1, POLES, PB, COLS), F32), ((1, PB, STEPS, COLS), F32))


def scratch(args):
    dma = pltpu.SemaphoreType.DMA
    return [pltpu.VMEM(a.shape, a.dtype) for a in args] + [
        pltpu.VMEM((128, 128), F32),
        pltpu.VMEM((2, SIDE, SIDE * PB, COLS), BF16),
        pltpu.VMEM((2, PB, COLS), F32),
        pltpu.VMEM((PB, 1024), BF16),
        pltpu.VMEM((SUBS, SLOT, 128), BF16),
        pltpu.VMEM((SUBS * SLOT, 256), BF16),
        dma((len(args),)),
        dma((5, 2, 4)),
        dma((5, 2, 4)),
        dma((SUBS,)),
        dma((SUBS,)),
        pltpu.SemaphoreType.REGULAR,
        pltpu.SemaphoreType.REGULAR,
    ]


def body(*args):
    args = list(args)
    for n in (5, 6):
        args[n] = args[n].reshape(POLES, 1, PB)
    args = [pltpu.with_memory_space_constraint(a, pltpu.HBM) for a in args]
    held = pl.pallas_call(
        kernel,
        out_shape=[pltpu.VMEM(s, d) for s, d in HELD],
        in_specs=[pl.BlockSpec(memory_space=pltpu.HBM)] * len(args),
        out_specs=[pl.BlockSpec(memory_space=pltpu.VMEM)] * 4,
        scratch_shapes=scratch(args),
        compiler_params=pltpu.CompilerParams(
            collective_id=0, has_side_effects=True, vmem_limit_bytes=32 * 1024 * 1024),
    )(*args)
    held = [pltpu.with_memory_space_constraint(a, pltpu.VMEM) for a in held]
    return pl.pallas_call(
        settle,
        out_shape=[pltpu.HBM(s, d) for s, d in OUTS],
        in_specs=[pl.BlockSpec(memory_space=pltpu.VMEM)] * 4,
        out_specs=[pl.BlockSpec(memory_space=pltpu.HBM)] * 3,
        scratch_shapes=[pltpu.VMEM(*OUTS[2]), pltpu.SemaphoreType.DMA((3,))],
    )(*held)


def solution(mesh):
    placed = (
        P("sub", "blk", None),
        P("sub", "blk"),
        P("sub", "blk"),
        P("sub", "blk"),
        P("sub", "blk"),
        P("sub", None, "blk"),
        P("sub", None, "blk"),
        P("sub", None, "blk", None),
        P("sub", None, "blk", None),
        P("sub", None),
        P("sub", None, None),
    )
    return jax.shard_map(
        body,
        mesh=mesh,
        in_specs=placed,
        out_specs=(P("sub", "blk", None), P("sub", None, "blk", None), P("sub", "blk", None, None)),
        check_vma=False,
    )
```

```python
import jax
import jax.numpy as jnp
from jax import lax
from jax.experimental import pallas as pl
from jax.experimental.pallas import tpu as pltpu
from jax.sharding import PartitionSpec as P

MESH = pl.DeviceIdType.MESH
F32, BF16, I32 = jnp.float32, jnp.bfloat16, jnp.int32

SUBS, SIDE, PB, NB, COLS, POLES, DEPTH, STEPS = 32, 4, 64, 1024, 256, 12, 4, 2
CAP = 6
SLOT = CAP * STEPS * 2
HOPS = (1, 3, 2)
NEAR = tuple((k, c) for k in (2, 14, 1, 15) for c in range(2)) + ((0, 1),)
WIDE = ((4, 0), (12, 0))


def turn_tables(blk, small, table):
    port_v, far_v, delay_v, adm_v, rate_v, res_v = small
    table[...] = jnp.zeros_like(table)
    table[0:POLES, 0:PB] = rate_v[:, 0, :]
    table[16:16 + POLES, 0:PB] = res_v[:, 0, :]
    table[32:33, 0:PB] = adm_v[...]
    table[33:34, 0:PB] = far_v[...].astype(F32)
    table[34:35, 0:PB] = (port_v[...] - blk * NB).astype(F32)
    table[35:36, 0:PB] = delay_v[...].astype(F32)
    table[...] = jnp.transpose(table[...])


def advance(x, y, table, state_v, hist_v, event_v, amp_v, new_v, source, gath):
    for part in range(4):
        rows = slice(part * 16, part * 16 + 16)
        delay = table[rows, 35:36]
        arrive = []
        for step in range(STEPS):
            got = jnp.zeros((16, COLS), F32)
            for d in range(DEPTH):
                got = jnp.where(delay == float(d + step + 1), hist_v[0, d, rows, :], got)
            arrive.append(got)
        totals = [jnp.zeros((16, COLS), F32) for _ in range(STEPS)]
        for p in range(POLES):
            rate = table[rows, p:p + 1]
            weight = table[rows, 16 + p:17 + p]
            now = state_v[0, p, rows, :]
            for step in range(STEPS):
                now = rate * now + weight * arrive[step]
                totals[step] = totals[step] + now
            new_v[0, p, rows, :] = now
        index = lax.broadcasted_iota(I32, (16, COLS), 0) + ((y * SIDE + x) * PB + part * 16)
        hit = event_v[...] == index
        for step in range(STEPS):
            source[step, rows, :] = totals[step]
            kick = jnp.where(hit, amp_v[0, step:step + 1, :], 0.0)
            gath[step, y, pl.ds(pl.multiple_of(x * PB + part * 16, 16), 16), :] = (totals[step] + kick).astype(BF16)


def places(far_v, table):
    far_row = far_v[...].astype(F32)
    far_col = table[0:PB, 33:34]
    same = far_col == far_row
    ii = lax.broadcasted_iota(I32, (PB, PB), 0)
    jj = lax.broadcasted_iota(I32, (PB, PB), 1)
    rank_row = jnp.sum(jnp.where(same & (ii < jj), 1.0, 0.0), axis=0, keepdims=True)
    rank_col = jnp.sum(jnp.where(same & (jj < ii), 1.0, 0.0), axis=1, keepdims=True)
    slot_row = (far_row * SLOT + rank_row).astype(I32)
    slot_col = (far_col * SLOT + rank_col).astype(I32)
    place_row = jnp.concatenate([slot_row + q * CAP for q in range(4)], axis=1)
    place_col = jnp.concatenate([slot_col + q * CAP for q in range(4)], axis=0)
    return place_row, place_col


def masks(far_v, table, pack, unpack):
    place_row, place_col = places(far_v, table)
    pack[...] = (lax.broadcasted_iota(I32, (SUBS * SLOT, 256), 0) == place_row).astype(BF16)
    unpack[...] = (lax.broadcasted_iota(I32, (256, SUBS * SLOT), 1) == place_col).astype(BF16)


def port_rows(table, z_v, ports):
    node_col = table[0:PB, 34:35].astype(I32)
    pick = (lax.broadcasted_iota(I32, (PB, NB), 1) == node_col).astype(BF16)
    ports[...] = jnp.dot(pick, z_v[0], preferred_element_type=F32).astype(BF16)


def waves_out(table, ports, gath, source, pack, outbox):
    twice = 2.0 * table[0:PB, 32:33]
    waves = []
    for t in range(2):
        volt = jnp.dot(ports[...], gath[t].reshape(1024, COLS), preferred_element_type=F32)
        wave = (twice * volt - source[t]).astype(BF16)
        waves += [wave[:, 0:128], wave[:, 128:256]]
    stacked = jnp.concatenate(waves, axis=0)
    boxes = jnp.dot(pack[...], stacked, preferred_element_type=F32).astype(BF16)
    outbox[...] = boxes.reshape(SUBS, SLOT, 128)


def peaks(z_v, gath, peak_ref, part):
    for part in (part,):
        rows = slice(part * 256, part * 256 + 256)
        v0 = jnp.dot(z_v[0, rows, :], gath[0].reshape(1024, COLS), preferred_element_type=F32)
        v1 = jnp.dot(z_v[0, rows, :], gath[1].reshape(1024, COLS), preferred_element_type=F32)
        peak_ref[0, rows, :] = jnp.maximum(jnp.abs(v0), jnp.abs(v1)).astype(BF16)


def spread(unpack, inbox, arr_ref):
    got = jnp.dot(unpack[...], inbox[...].reshape(SUBS * SLOT, 128), preferred_element_type=F32)
    for t in range(2):
        arr_ref[0, :, t, 0:128] = got[128 * t:128 * t + PB]
        arr_ref[0, :, t, 128:256] = got[128 * t + PB:128 * t + 2 * PB]


def kernel(
    z_hbm, port_hbm, far_hbm, delay_hbm, adm_hbm, rate_hbm, res_hbm, state_hbm, hist_hbm, event_hbm, amp_hbm,
    peak_ref, new_ref, inbox, unpack,
    z_v, port_v, far_v, delay_v, adm_v, rate_v, res_v, state_v, hist_v, event_v, amp_v,
    table, gath, source, ports, outbox, pack,
    in_sem, ring_s, ring_r, out_sem, box_sem, met, wide,
):
    sub = lax.axis_index("sub")
    blk = lax.axis_index("blk")
    x = lax.rem(blk, SIDE)
    y = lax.div(blk, SIDE)

    def along(axis, k):
        if axis == 0:
            return y, lax.rem(x + k, SIDE)
        return lax.rem(y + k, SIDE), x

    barrier = pltpu.get_barrier_semaphore()
    for axis in range(2):
        for k in (2, 1, 3):
            py, px = along(axis, k)
            pl.semaphore_signal(barrier, inc=1, device_id=(sub, py * SIDE + px), device_id_type=MESH)

    chip, core = lax.div(sub, 2), lax.rem(sub, 2)

    def tell(sem, offsets):
        for k, c in offsets:
            peer = lax.rem(chip + k, SUBS // 2) * 2 + lax.rem(core + c, 2)
            pl.semaphore_signal(sem, inc=1, device_id=(peer, blk), device_id_type=MESH)

    tell(barrier, NEAR)

    loads = []
    pairs = (
        (port_hbm, port_v), (far_hbm, far_v), (delay_hbm, delay_v), (adm_hbm, adm_v), (rate_hbm, rate_v),
        (res_hbm, res_v), (event_hbm, event_v), (amp_hbm, amp_v), (hist_hbm, hist_v), (state_hbm, state_v), (z_hbm, z_v),
    )
    for n, (src, dst) in enumerate(pairs):
        loads.append(pltpu.make_async_copy(src, dst, in_sem.at[n]))
        if n < 10:
            loads[n].start()

    for n in range(8):
        loads[n].wait()
    turn_tables(blk, (port_v, far_v, delay_v, adm_v, rate_v, res_v), table)
    loads[8].wait()
    loads[9].wait()
    loads[10].start()
    advance(x, y, table, state_v, hist_v, event_v, amp_v, new_ref, source, gath)

    pl.semaphore_wait(barrier, 6 + len(NEAR))

    sent = []

    def slab(t, yy, xx, axis, k, lo=0, size=PB):
        n = len(sent)
        ref = gath.at[t, yy, pl.ds(pl.multiple_of(xx * PB + lo, 16), size), :]
        py, px = along(axis, k)
        c = pltpu.make_async_remote_copy(
            src_ref=ref, dst_ref=ref, send_sem=ring_s.at[n], recv_sem=ring_r.at[n],
            device_id=(sub, py * SIDE + px), device_id_type=MESH)
        c.start()
        sent.append(c)
        return c

    def between():
        tell(met, NEAR)
        masks(far_v, table, pack, unpack)

    def between2():
        pl.semaphore_wait(met, len(NEAR))
        tell(wide, WIDE)
    line = {(t, k): slab(t, y, x, t, k) for k in (2, 1, 3) for t in range(2)}
    last = [slab(t, y, x, 1 - t, j) for t in range(2) for j in (2, 1, 3)]
    between()
    for k in (1, 3, 2):
        for t in range(2):
            line[t, k].wait_recv()
            yy, xx = along(t, SIDE - k)
            last += [slab(t, yy, xx, 1 - t, j) for j in (2, 1, 3)]
        if k == 3:
            between2()
    loads[10].wait()
    port_rows(table, z_v, ports)
    for c in last:
        c.wait_recv()

    waves_out(table, ports, gath, source, pack, outbox)
    pl.semaphore_wait(wide, len(WIDE))

    def box(k):
        d = lax.rem(sub + k, SUBS)
        return pltpu.make_async_remote_copy(
            src_ref=outbox.at[d], dst_ref=inbox.at[sub], send_sem=out_sem.at[d], recv_sem=box_sem.at[sub],
            device_id=(d, blk), device_id_type=MESH)

    def post(i, c):
        box(lax.rem(i + SUBS - sub, SUBS)).start()
        return c

    for part in range(4):
        lo = part * 8
        lax.fori_loop(lo, jnp.clip(sub, lo, lo + 8), post, 0)
        lax.fori_loop(jnp.clip(sub + 1, lo, lo + 8), lo + 8, post, 0)
        peaks(z_v, gath, peak_ref, part)
    inbox[sub] = jnp.zeros((SLOT, 128), BF16)

    for c in sent:
        c.wait_send()

    def drain(k, c):
        box(k).wait_send()
        return c

    lax.fori_loop(1, SUBS, drain, 0)

    def arrived(d):
        pltpu.make_async_remote_copy(
            src_ref=outbox.at[d], dst_ref=inbox.at[d], send_sem=out_sem.at[d], recv_sem=box_sem.at[d],
            device_id=(d, blk), device_id_type=MESH).wait_recv()

    arrived(chip * 2 + 1 - core)

    def collect(k, c):
        for far in (k, SUBS // 2 - k):
            for side in range(2):
                arrived(lax.rem(chip + far, SUBS // 2) * 2 + side)
        return c

    lax.fori_loop(1, SUBS // 4, collect, 0)
    for side in range(2):
        arrived(lax.rem(chip + SUBS // 4, SUBS // 2) * 2 + side)


def settle(peak, new, inbox, unpack, peak_hbm, new_hbm, arr_hbm, arr, sem):
    copies = [pltpu.make_async_copy(a, b, sem.at[n]) for n, (a, b) in enumerate(((peak, peak_hbm), (new, new_hbm), (arr, arr_hbm)))]
    copies[0].start()
    copies[1].start()
    spread(unpack, inbox, arr)
    copies[2].start()
    for q in copies:
        q.wait()


HELD = (
    ((1, NB, COLS), BF16), ((1, POLES, PB, COLS), F32), ((SUBS, SLOT, 128), BF16), ((256, SUBS * SLOT), BF16),
)
OUTS = (((1, NB, COLS), BF16), ((1, POLES, PB, COLS), F32), ((1, PB, STEPS, COLS), F32))


def scratch(args):
    dma = pltpu.SemaphoreType.DMA
    return [pltpu.VMEM(a.shape, a.dtype) for a in args] + [
        pltpu.VMEM((128, 128), F32),
        pltpu.VMEM((2, SIDE, SIDE * PB, COLS), BF16),
        pltpu.VMEM((2, PB, COLS), F32),
        pltpu.VMEM((PB, 1024), BF16),
        pltpu.VMEM((SUBS, SLOT, 128), BF16),
        pltpu.VMEM((SUBS * SLOT, 256), BF16),
        dma((len(args),)),
        dma((40,)),
        dma((40,)),
        dma((SUBS,)),
        dma((SUBS,)),
        pltpu.SemaphoreType.REGULAR,
        pltpu.SemaphoreType.REGULAR,
    ]


def body(*args):
    args = list(args)
    for n in (5, 6):
        args[n] = args[n].reshape(POLES, 1, PB)
    args = [pltpu.with_memory_space_constraint(a, pltpu.HBM) for a in args]
    held = pl.pallas_call(
        kernel,
        out_shape=[pltpu.VMEM(s, d) for s, d in HELD],
        in_specs=[pl.BlockSpec(memory_space=pltpu.HBM)] * len(args),
        out_specs=[pl.BlockSpec(memory_space=pltpu.VMEM)] * 4,
        scratch_shapes=scratch(args),
        compiler_params=pltpu.CompilerParams(
            collective_id=0, has_side_effects=True, vmem_limit_bytes=32 * 1024 * 1024),
    )(*args)
    held = [pltpu.with_memory_space_constraint(a, pltpu.VMEM) for a in held]
    return pl.pallas_call(
        settle,
        out_shape=[pltpu.HBM(s, d) for s, d in OUTS],
        in_specs=[pl.BlockSpec(memory_space=pltpu.VMEM)] * 4,
        out_specs=[pl.BlockSpec(memory_space=pltpu.HBM)] * 3,
        scratch_shapes=[pltpu.VMEM(*OUTS[2]), pltpu.SemaphoreType.DMA((3,))],
    )(*held)


def solution(mesh):
    placed = (
        P("sub", "blk", None),
        P("sub", "blk"),
        P("sub", "blk"),
        P("sub", "blk"),
        P("sub", "blk"),
        P("sub", None, "blk"),
        P("sub", None, "blk"),
        P("sub", None, "blk", None),
        P("sub", None, "blk", None),
        P("sub", None),
        P("sub", None, None),
    )
    return jax.shard_map(
        body,
        mesh=mesh,
        in_specs=placed,
        out_specs=(P("sub", "blk", None), P("sub", None, "blk", None), P("sub", "blk", None, None)),
        check_vma=False,
    )
```
